512 devices in a mesh: kvp: 64 (over z, y), tp: 8 (over x, core).
Axes of the slice: x: 4, y: 4, z: 16, core: 2. Of those that a mesh axis runs over, the one named last changes fastest.
Arguments:
- query: bfloat16 [4, 128, 128], P(None, 'tp'), may hold values from -1000 to 1000
- key_cache: bfloat16 [4, 8, 16384, 128], P(None, 'tp', 'kvp'), may hold values from -4 to 4
- value_cache: bfloat16 [4, 8, 16384, 128], P(None, 'tp', 'kvp'), may hold values from -6 to 6
- lengths: int32 [4], replicated, may hold values from 2048 to 16384, as said below
- out_weight: bfloat16 [16384, 16384], P('tp', 'kvp'), may hold values from -0.046875 to 0.046875
- residual: bfloat16 [4, 16384], P(None, 'kvp'), may hold values from -0.3125 to 0.3125
- norm_gain: float32 [16384], P('kvp'), may hold values from 0.5 to 1.5
- gate_weight: bfloat16 [16384, 26624], P('kvp', 'tp'), may hold values from -0.046875 to 0.046875
- up_weight: bfloat16 [16384, 26624], P('kvp', 'tp'), may hold values from -0.046875 to 0.046875
Outputs:
- stream: bfloat16 [4, 16384], P(None, 'kvp')
- hidden: bfloat16 [4, 26624], P(None, 'tp')
The draws below stay inside these ranges and needn't reach their ends.
Inputs may be any that keep to these rules, and one draw needn't show every extreme that they name: `lengths`: at least one sequence has exactly 16384 live positions and one has exactly 2048.
All inputs are finite; a program needn't handle non-finite values.
Results may differ from the reference program's by a relative error of at most 0.028.
Values may be sent and summed in bfloat16 or wider, within the bound.
No kernel may reach another device: no remote copies, remote signals or barrier semaphores. Data moves between devices by JAX's collectives and lax.ppermute only.
A program may use at most 64 MiB of HBM per device.

```python
import jax
import jax.numpy as jnp
from jax import lax

ROWS = 4
D = 16384
HEADS = 128
KV_HEADS = 8
HEAD_DIM = 128
FF = 26624
CONTEXT = 16384


def drawn_keys(key):
    normal_keys = jax.random.normal(jax.random.fold_in(key, 11), (ROWS, KV_HEADS, CONTEXT, HEAD_DIM), jnp.float32)
    return jnp.clip(normal_keys, -4.0, 4.0)


def draw_key_cache(key, part):
    base = drawn_keys(key)
    return base.astype(jnp.bfloat16)


def draw_query(key, part):
    key = jax.random.fold_in(key, 5)
    groups = HEADS // KV_HEADS
    entries = jax.random.normal(key, (ROWS, KV_HEADS, groups, HEAD_DIM), jnp.float32)
    return entries.reshape(ROWS, HEADS, HEAD_DIM).astype(jnp.bfloat16)


def draw_lengths(key, part):
    key = jax.random.fold_in(key, 7)
    drawn = jax.random.randint(key, (ROWS,), CONTEXT // 8, CONTEXT + 1)
    longest = jax.random.randint(jax.random.fold_in(key, 1), (), 0, ROWS)
    row_ids = jnp.arange(ROWS, dtype=jnp.int32)
    drawn = jnp.where(row_ids == longest, CONTEXT, drawn)
    drawn = jnp.where(row_ids == (longest + 1) % ROWS, CONTEXT // 8, drawn)
    return drawn.astype(jnp.int32)


def block_levels(rng, shape, cuts, least, largest):
    def one(axis_at, shards_of):
        draws = jax.random.uniform(jax.random.fold_in(jax.random.fold_in(rng, 6), axis_at), (shards_of,), jnp.float32, least / len(cuts), largest / len(cuts))
        return jnp.repeat(jnp.exp(draws), shape[axis_at] // shards_of).reshape((-1,) + (1,) * (len(shape) - axis_at - 1))

    gain = one(*cuts[0])
    for cut in cuts[1:]:
        gain = gain * one(*cut)
    return gain


def scatter_about(rng, extent, deviation, limit, split=(), held_as=jnp.bfloat16):
    result = deviation * jax.random.normal(rng, extent, jnp.float32)
    if split:
        result = result * block_levels(rng, extent, split, -0.22, 0.18)
    return jnp.clip(result, -limit, limit).astype(held_as)


def setup_inputs(seed: int = 0) -> dict:
    streams_of = jax.random.split(jax.random.key(seed), 10)
    return {
        "query": draw_query(jax.random.fold_in(streams_of[9], 71), 0),
        "key_cache": draw_key_cache(jax.random.fold_in(streams_of[9], 71), 0),
        "value_cache": scatter_about(streams_of[2], (ROWS, KV_HEADS, CONTEXT, HEAD_DIM), 1.0, 6.0, ((1, 8), (2, 64))),
        "lengths": draw_lengths(jax.random.fold_in(streams_of[9], 71), 0),
        "out_weight": scatter_about(streams_of[4], (HEADS * HEAD_DIM, D), (HEADS * HEAD_DIM) ** -0.5, 0.046875, ((0, 8), (1, 64))),
        "residual": scatter_about(streams_of[5], (ROWS, D), 0.02, 0.3125, ((1, 64),)),
        "norm_gain": jnp.clip(1.0 + 0.1 * jax.random.normal(streams_of[6], (D,), jnp.float32), 0.5, 1.5),
        "gate_weight": scatter_about(streams_of[7], (D, FF), D ** -0.5, 0.046875, ((0, 64), (1, 8))),
        "up_weight": scatter_about(streams_of[8], (D, FF), D ** -0.5, 0.046875, ((0, 64), (1, 8))),
    }


def reference(query, key_cache, value_cache, lengths, out_weight, residual, norm_gain, gate_weight, up_weight):
    groups = HEADS // KV_HEADS
    queries = query.astype(jnp.float32).reshape(ROWS, KV_HEADS, groups, HEAD_DIM)
    scores = jnp.einsum('rkgd,rkpd->rkgp', queries, key_cache.astype(jnp.float32)) * HEAD_DIM ** (-0.5)
    positions = jnp.arange(CONTEXT, dtype=jnp.int32)
    is_valid = (positions[None, :] < lengths[:, None])[:, None, None, :]
    masked = jnp.where(is_valid, scores, -1e+30)
    top_score = lax.optimization_barrier(jnp.max(masked, axis=-1, keepdims=True))
    weights = jnp.where(is_valid, jnp.exp(masked - top_score), 0.0)
    weight_sum = lax.optimization_barrier(jnp.sum(weights, axis=-1))
    rounded = lax.optimization_barrier(weights.astype(jnp.bfloat16)).astype(jnp.float32)
    summed = jnp.einsum('rkgp,rkpd->rkgd', rounded, value_cache.astype(jnp.float32))
    attention = (summed / weight_sum[..., None]).reshape(ROWS, HEADS * HEAD_DIM).astype(jnp.bfloat16)
    mixed = residual.astype(jnp.float32) + jnp.dot(attention, out_weight, preferred_element_type=jnp.float32)
    mean_square = lax.optimization_barrier(jnp.mean(mixed * mixed, axis=1, keepdims=True))
    normed = (mixed * lax.rsqrt(mean_square + 1e-05) * norm_gain).astype(jnp.bfloat16)
    gate_sum = jnp.dot(normed, gate_weight, preferred_element_type=jnp.float32)
    up_sum = jnp.dot(normed, up_weight, preferred_element_type=jnp.float32)
    hidden = (jax.nn.silu(gate_sum) * up_sum).astype(jnp.bfloat16)
    return (mixed.astype(jnp.bfloat16), hidden)
```

```python
import jax
import jax.numpy as jnp
from jax import lax
from jax.sharding import Mesh
from jax.sharding import PartitionSpec as P

NEAR = 8
LANES = 128


def spread(block, axis):
    count = lax.axis_size(axis)
    copies = jnp.broadcast_to(block[None], (count,) + block.shape)
    return lax.all_to_all(copies, axis, 0, 0, tiled=True)


def split_pair(value):
    high = value.astype(jnp.bfloat16)
    low = (value - high.astype(jnp.float32)).astype(jnp.bfloat16)
    return high, low


def pack(out, peak, total):
    stats = jnp.stack(split_pair(peak) + split_pair(total))
    stats = jnp.pad(stats, ((0, 12), (0, LANES - stats.shape[1])))
    return jnp.concatenate([out.astype(jnp.bfloat16), stats])


def combine(blocks):
    pairs = blocks.shape[1] - 16
    out = blocks[:, :pairs].astype(jnp.float32)
    stats = blocks[:, pairs:, :pairs].astype(jnp.float32)
    peaks = stats[:, 0] + stats[:, 1]
    totals = stats[:, 2] + stats[:, 3]
    peak = jnp.max(peaks, axis=0)
    factor = jnp.exp(peaks - peak[None])
    return jnp.sum(out * factor[..., None], axis=0), peak, jnp.sum(totals * factor, axis=0)


def local(
    query, key_cache, value_cache, lengths, out_weight, residual, norm_gain, gate_weight, up_weight
):
    rows, heads, head_dim = query.shape
    span = key_cache.shape[2]
    scores = jnp.einsum(
        "rgd,rpd->rgp", query, key_cache[:, 0], preferred_element_type=jnp.float32
    ) * head_dim ** (-0.5)
    block = lax.axis_index("far") * lax.axis_size("near") + lax.axis_index("near")
    positions = block * span + jnp.arange(span, dtype=jnp.int32)
    is_valid = (positions[None, :] < lengths[:, None])[:, None, :]
    masked = jnp.where(is_valid, scores, -1e30)
    high, low = split_pair(jnp.max(masked, axis=-1))
    peak = high.astype(jnp.float32) + low.astype(jnp.float32)
    weights = jnp.where(is_valid, jnp.exp(masked - peak[..., None]), 0.0)
    total = jnp.sum(weights, axis=-1)
    out = jnp.einsum(
        "rgp,rpd->rgd", weights.astype(jnp.bfloat16), value_cache[:, 0],
        preferred_element_type=jnp.float32,
    )
    state = (out.reshape(rows * heads, head_dim), peak.reshape(-1), total.reshape(-1))
    state = combine(spread(pack(*state), "near"))
    out, _, total = combine(spread(pack(*state), "far"))
    attention = (out / total[:, None]).astype(jnp.bfloat16).reshape(rows, heads * head_dim)
    projected = jnp.dot(attention, out_weight, preferred_element_type=jnp.float32)
    mixed = residual.astype(jnp.float32) + jnp.sum(spread(projected, "tp"), axis=0)
    squares = jnp.sum(mixed * mixed, axis=1)
    scaled = (mixed * norm_gain).astype(jnp.bfloat16)
    gate_part = jnp.dot(scaled, gate_weight, preferred_element_type=jnp.float32)
    up_part = jnp.dot(scaled, up_weight, preferred_element_type=jnp.float32)
    width = gate_part.shape[1]
    halves = NEAR // rows
    deep = width // halves // LANES
    tail = 32 - 2 * deep - 2

    def ending(value):
        pair = jnp.stack(split_pair(value), axis=-1)[..., None]
        pair = jnp.broadcast_to(pair, pair.shape[:-1] + (LANES,))
        return jnp.pad(pair, ((0, 0),) * (pair.ndim - 2) + ((0, tail), (0, 0)))

    terms = jnp.concatenate(
        [
            gate_part.astype(jnp.bfloat16).reshape(NEAR, deep, LANES),
            up_part.astype(jnp.bfloat16).reshape(NEAR, deep, LANES),
            ending(jnp.repeat(squares, halves)),
        ],
        axis=1,
    )
    terms = lax.all_to_all(terms, "near", 0, 0, tiled=True)
    terms = jnp.sum(terms.astype(jnp.float32), axis=0)
    squares = (terms[2 * deep] + terms[2 * deep + 1])[0]
    terms = jnp.concatenate([terms[: 2 * deep].astype(jnp.bfloat16), ending(squares)])
    terms = jnp.sum(spread(terms, "far").astype(jnp.float32), axis=0)
    squares = terms[2 * deep] + terms[2 * deep + 1]
    features = mixed.shape[1] * lax.axis_size("far") * lax.axis_size("near")
    inv_rms = lax.rsqrt(squares / features + 1e-05)
    gate_sum = terms[:deep] * inv_rms
    up_sum = terms[deep : 2 * deep] * inv_rms
    hidden = (jax.nn.silu(gate_sum) * up_sum).astype(jnp.bfloat16)
    hidden = spread(hidden, "near").reshape(rows, width)
    return (mixed.astype(jnp.bfloat16), hidden)


def solution(mesh):
    far = mesh.shape["kvp"] // NEAR
    devices = mesh.devices.reshape(far, NEAR, mesh.shape["tp"])
    inner = Mesh(devices, ("far", "near", "tp"))
    kvp = ("far", "near")
    placed = (
        P(None, "tp", None),
        P(None, "tp", kvp, None),
        P(None, "tp", kvp, None),
        P(),
        P("tp", kvp),
        P(None, kvp),
        P(kvp),
        P(kvp, "tp"),
        P(kvp, "tp"),
    )
    return jax.shard_map(
        local,
        mesh=inner,
        in_specs=placed,
        out_specs=(P(None, kvp), P(None, "tp")),
        check_vma=False,
    )
```

```python
import jax
import jax.numpy as jnp
from jax import lax
from jax.experimental import pallas as pl
from jax.experimental.pallas import tpu as pltpu
from jax.sharding import Mesh
from jax.sharding import PartitionSpec as P

NEAR = 8
LANES = 128


def spread(block, axis):
    count = lax.axis_size(axis)
    copies = jnp.broadcast_to(block[None], (count,) + block.shape)
    return lax.all_to_all(copies, axis, 0, 0, tiled=True)


def split_pair(value):
    high = lax.reduce_precision(value, 8, 7)
    low = lax.reduce_precision(value - high, 8, 7)
    return high, low


def pack(out, stats):
    return jnp.concatenate([out.astype(jnp.bfloat16), stats.astype(jnp.bfloat16)])


def combine(blocks):
    pairs = blocks.shape[1] - 8
    out = blocks[:, :pairs].astype(jnp.float32)
    stats = blocks[:, pairs:, :pairs].astype(jnp.float32)
    peaks = stats[:, 0] + stats[:, 1]
    totals = stats[:, 2] + stats[:, 3]
    peak = jnp.max(peaks, axis=0)
    factor = jnp.exp(peaks - peak[None])
    total = jnp.sum(totals * factor, axis=0)
    return jnp.sum(out * factor[..., None], axis=0), peak, total


def stacked(peak, total):
    stats = jnp.stack(split_pair(peak) + split_pair(total))
    return jnp.pad(stats, ((0, 4), (0, LANES - stats.shape[1])))


def halves_of(value):
    high = value.astype(jnp.bfloat16).astype(jnp.float32)
    return high, value - high


def attend(
    lengths_hbm, query_hbm, key_hbm, value_hbm, *others,
):
    count = (len(others) - 7) // 2
    out_ref, stats_ref, *fetched = others[count : 2 * count + 2]
    lengths_ref, query_ref, key_ref, value_ref, arrived = others[2 * count + 2 :]
    sources = (lengths_hbm, query_hbm, key_hbm, value_hbm, *others[:count])
    targets = (lengths_ref, query_ref, key_ref, value_ref, *fetched)
    copies = [
        pltpu.make_async_copy(source, target, arrived.at[at])
        for at, (source, target) in enumerate(zip(sources, targets))
    ]
    for copy in copies:
        copy.start()
    rows, heads, head_dim = query_ref.shape
    span = key_ref.shape[2]
    block = lax.axis_index("far") * NEAR + lax.axis_index("near")
    positions = block * span + lax.broadcasted_iota(jnp.int32, (heads, span), 1)
    lane = lax.broadcasted_iota(jnp.int32, (rows * heads, LANES), 1)
    for copy in copies[:3]:
        copy.wait()
    scores = [
        lax.dot_general(
            query_ref[row], key_ref[row, 0], (((1,), (1,)), ((), ())),
            preferred_element_type=jnp.float32,
        )
        for row in range(rows)
    ]
    live = jnp.concatenate([positions < lengths_ref[row] for row in range(rows)])
    masked = jnp.where(live, jnp.concatenate(scores) * head_dim ** (-0.5), -1e30)
    top = jnp.max(masked, axis=1, keepdims=True)
    high, low = halves_of(top)
    low = low.astype(jnp.bfloat16).astype(jnp.float32)
    weights = jnp.where(live, jnp.exp(masked - (high + low)), 0.0)
    rounded = weights.astype(jnp.bfloat16)
    copies[3].wait()
    for row in range(rows):
        out_ref[row] = jnp.dot(
            rounded[row * heads : (row + 1) * heads], value_ref[row, 0],
            preferred_element_type=jnp.float32,
        ).astype(jnp.bfloat16)
    total_high, total_low = halves_of(jnp.sum(weights, axis=1, keepdims=True))
    stats = jnp.where(lane == 0, high, jnp.where(lane == 1, low, 0.0))
    stats = jnp.where(lane == 2, total_high, jnp.where(lane == 3, total_low, stats))
    empty = jnp.zeros((LANES - rows * heads, LANES), jnp.float32)
    stats_ref[...] = jnp.concatenate([stats, empty]).T[:8]
    for copy in copies[4:]:
        copy.wait()


def project(blocks_ref, weight_ref, out_ref, attention_ref):
    count = blocks_ref.shape[0]
    pairs = attention_ref.shape[0]
    rows = out_ref.shape[0]
    heads = pairs // rows
    blocks = [blocks_ref[at].astype(jnp.float32) for at in range(count)]
    stats = [block[pairs : pairs + 8] for block in blocks]
    peaks = [stat[0:1] + stat[1:2] for stat in stats]
    peak = peaks[0]
    for other in peaks[1:]:
        peak = jnp.maximum(peak, other)
    factors = [jnp.exp(other - peak) for other in peaks]
    lane = lax.broadcasted_iota(jnp.int32, (1, LANES), 1)
    total = jnp.where(lane < pairs, 0.0, 1.0)
    for factor, stat in zip(factors, stats):
        total = total + factor * (stat[2:3] + stat[3:4])
    factors = jnp.concatenate([factor / total for factor in factors])
    empty = jnp.zeros((LANES - count, LANES), jnp.float32)
    columns = jnp.concatenate([factors, empty]).T
    attention = blocks[0][:pairs] * columns[:pairs, 0:1]
    for at in range(1, count):
        attention = attention + blocks[at][:pairs] * columns[:pairs, at : at + 1]
    attention_ref[...] = attention
    attention = jnp.concatenate(
        [attention_ref[pl.ds(head, rows, stride=heads), :] for head in range(heads)], axis=1
    ).astype(jnp.bfloat16)
    out_ref[...] = jnp.dot(attention, weight_ref[...], preferred_element_type=jnp.float32)


def feed(terms_ref, residual_ref, gain_ref, gate_ref, up_ref, mixed_ref, wide_ref):
    mixed = residual_ref[...].astype(jnp.float32)
    for at in range(terms_ref.shape[0]):
        mixed = mixed + terms_ref[at]
    mixed_ref[...] = mixed
    rows = mixed.shape[0]
    halves = NEAR // rows
    deep = gate_ref.shape[1] // halves // LANES
    squares = jnp.sum(mixed * mixed, axis=1, keepdims=True)
    high, low = halves_of(jnp.broadcast_to(squares, (rows, LANES)))
    wide_ref[...] = jnp.zeros_like(wide_ref)
    for half in range(halves):
        wide_ref[pl.ds(half, rows, stride=halves), 2 * deep, :] = high
        wide_ref[pl.ds(half, rows, stride=halves), 2 * deep + 1, :] = low
    scaled = (mixed * gain_ref[...]).astype(jnp.bfloat16)
    for first, weight_ref in ((0, gate_ref), (deep, up_ref)):
        terms = jnp.dot(scaled, weight_ref[...], preferred_element_type=jnp.float32)
        for half in range(halves):
            for at in range(deep):
                column = (half * deep + at) * LANES
                piece = terms[:, column : column + LANES]
                wide_ref[pl.ds(half, rows, stride=halves), first + at, :] = piece


def finish(mixed_ref, blocks_ref, stream_hbm, hidden_hbm, wide_ref, stream_ref, hidden_ref, sent):
    stream_ref[...] = mixed_ref[...].astype(jnp.bfloat16)
    first = pltpu.make_async_copy(stream_ref, stream_hbm, sent.at[0])
    first.start()
    rows = stream_ref.shape[0]
    halves = NEAR // rows
    deep = blocks_ref.shape[1]
    wide_ref[...] = blocks_ref[...].astype(jnp.float32)
    for half in range(halves):
        for at in range(deep):
            piece = wide_ref[pl.ds(half, rows, stride=halves), at, :]
            column = (half * deep + at) * LANES
            hidden_ref[:, column : column + LANES] = piece.astype(jnp.bfloat16)
    second = pltpu.make_async_copy(hidden_ref, hidden_hbm, sent.at[1])
    second.start()
    first.wait()
    second.wait()


def local(
    query, key_cache, value_cache, lengths, out_weight, residual, norm_gain, gate_weight, up_weight
):
    rows, heads, head_dim = query.shape
    vmem, hbm = pl.BlockSpec(memory_space=pltpu.VMEM), pl.BlockSpec(memory_space=pltpu.HBM)
    params = pltpu.CompilerParams(vmem_limit_bytes=16 * 2**20)
    sources = (lengths, query, key_cache, value_cache, up_weight)
    out, stats, up_weight = pl.pallas_call(
        attend,
        out_shape=(
            pltpu.VMEM((rows, heads, head_dim), jnp.bfloat16),
            pltpu.VMEM((8, LANES), jnp.float32),
            pltpu.VMEM(up_weight.shape, jnp.bfloat16),
        ),
        in_specs=[hbm] * len(sources),
        out_specs=(vmem,) * 3,
        scratch_shapes=[
            pltpu.SMEM(lengths.shape, jnp.int32),
            pltpu.VMEM(query.shape, jnp.bfloat16),
            pltpu.VMEM(key_cache.shape, jnp.bfloat16),
            pltpu.VMEM(value_cache.shape, jnp.bfloat16),
            pltpu.SemaphoreType.DMA((len(sources),)),
        ],
        compiler_params=params,
    )(*[pltpu.with_memory_space_constraint(source, pltpu.HBM) for source in sources])
    out = out.reshape(rows * heads, head_dim)
    out, peak, total = combine(spread(pack(out, stats), "near"))
    blocks = spread(pack(out, stacked(peak, total)), "far")
    block_width = out_weight.shape[1]
    projected = pl.pallas_call(
        project,
        out_shape=jax.ShapeDtypeStruct((rows, block_width), jnp.float32),
        in_specs=[vmem] * 2,
        out_specs=vmem,
        scratch_shapes=[pltpu.VMEM((rows * heads, head_dim), jnp.float32)],
        compiler_params=params,
    )(blocks, out_weight)
    width = gate_weight.shape[1]
    halves = NEAR // rows
    deep = width // halves // LANES
    tall = -(-(2 * deep + 2) // 16) * 16
    mixed, terms = pl.pallas_call(
        feed,
        out_shape=(
            pltpu.VMEM((rows, block_width), jnp.float32),
            pltpu.VMEM((NEAR, tall, LANES), jnp.float32),
        ),
        in_specs=[vmem] * 5,
        out_specs=(vmem,) * 2,
        compiler_params=params,
    )(spread(projected, "tp"), residual, norm_gain.reshape(1, -1), gate_weight, up_weight)

    terms = lax.all_to_all(terms.astype(jnp.bfloat16), "near", 0, 0, tiled=True)
    terms = jnp.sum(terms.astype(jnp.float32), axis=0)
    pair = jnp.stack(split_pair(terms[2 * deep] + terms[2 * deep + 1]))
    terms = jnp.concatenate([terms[: 2 * deep], pair, terms[2 * deep + 2 :]]).astype(jnp.bfloat16)
    terms = jnp.sum(spread(terms, "far").astype(jnp.float32), axis=0)
    features = block_width * lax.axis_size("far") * lax.axis_size("near")
    mean_square = (terms[2 * deep] + terms[2 * deep + 1]) / features
    inv_rms = lax.rsqrt(mean_square + 1e-05)
    gate_sum = terms[:deep] * inv_rms
    up_sum = terms[deep : 2 * deep] * inv_rms
    hidden = (jax.nn.silu(gate_sum) * up_sum).astype(jnp.bfloat16)
    blocks = spread(hidden, "near")
    return tuple(pl.pallas_call(
        finish,
        out_shape=(
            jax.ShapeDtypeStruct((rows, block_width), jnp.bfloat16),
            jax.ShapeDtypeStruct((rows, width), jnp.bfloat16),
        ),
        in_specs=[vmem] * 2,
        out_specs=(hbm, hbm),
        scratch_shapes=[
            pltpu.VMEM(blocks.shape, jnp.float32),
            pltpu.VMEM((rows, block_width), jnp.bfloat16),
            pltpu.VMEM((rows, width), jnp.bfloat16),
            pltpu.SemaphoreType.DMA((2,)),
        ],
        compiler_params=params,
    )(mixed, blocks))


def solution(mesh):
    far = mesh.shape["kvp"] // NEAR
    devices = mesh.devices.reshape(far, NEAR, mesh.shape["tp"])
    inner = Mesh(devices, ("far", "near", "tp"))
    kvp = ("far", "near")
    placed = (
        P(None, "tp", None),
        P(None, "tp", kvp, None),
        P(None, "tp", kvp, None),
        P(),
        P("tp", kvp),
        P(None, kvp),
        P(kvp),
        P(kvp, "tp"),
        P(kvp, "tp"),
    )
    return jax.shard_map(
        local,
        mesh=inner,
        in_specs=placed,
        out_specs=(P(None, kvp), P(None, "tp")),
        check_vma=False,
    )
```

```python
import jax
import jax.numpy as jnp
from jax import lax
from jax.experimental import pallas as pl
from jax.experimental.pallas import tpu as pltpu
from jax.sharding import PartitionSpec as P

NEAR = 8
LANES = 128


def teams(count):
    near = []
    for first in range(0, count, NEAR):
        turn = NEAR // 2 if 2 * first >= count else 0
        near.append([first + (at ^ turn) for at in range(NEAR)])
    return near, [list(far) for far in zip(*near)]


def exchange(blocks, axis, groups=None):
    return lax.all_to_all(blocks, axis, 0, 0, axis_index_groups=groups, tiled=True)


def spread(block, axis, groups=None):
    count = len(groups[0]) if groups else lax.axis_size(axis)
    return exchange(jnp.broadcast_to(block[None], (count,) + block.shape), axis, groups)


def split_pair(value):
    high = lax.reduce_precision(value, 8, 7)
    low = lax.reduce_precision(value - high, 8, 7)
    return high, low


def pack(out, stats):
    return jnp.concatenate([out.astype(jnp.bfloat16), stats.astype(jnp.bfloat16)])


def combine(blocks):
    pairs = blocks.shape[1] - 8
    out = blocks[:, :pairs].astype(jnp.float32)
    stats = blocks[:, pairs:, :pairs].astype(jnp.float32)
    peaks = stats[:, 0] + stats[:, 1]
    totals = stats[:, 2] + stats[:, 3]
    peak = jnp.max(peaks, axis=0)
    factor = jnp.exp(peaks - peak[None])
    total = jnp.sum(totals * factor, axis=0)
    return jnp.sum(out * factor[..., None], axis=0), peak, total


def stacked(peak, total):
    stats = jnp.stack(split_pair(peak) + split_pair(total))
    return jnp.pad(stats, ((0, 4), (0, LANES - stats.shape[1])))


def halves_of(value):
    high = value.astype(jnp.bfloat16).astype(jnp.float32)
    return high, value - high


def attend(
    lengths_hbm, query_hbm, key_hbm, value_hbm, *others,
):
    count = (len(others) - 7) // 2
    out_ref, stats_ref, *fetched = others[count : 2 * count + 2]
    lengths_ref, query_ref, key_ref, value_ref, arrived = others[2 * count + 2 :]
    sources = (lengths_hbm, query_hbm, key_hbm, value_hbm, *others[:count])
    targets = (lengths_ref, query_ref, key_ref, value_ref, *fetched)
    copies = [
        pltpu.make_async_copy(source, target, arrived.at[at])
        for at, (source, target) in enumerate(zip(sources, targets))
    ]
    for copy in copies:
        copy.start()
    rows, heads, head_dim = query_ref.shape
    span = key_ref.shape[2]
    block = lax.axis_index("kvp")
    positions = block * span + lax.broadcasted_iota(jnp.int32, (heads, span), 1)
    lane = lax.broadcasted_iota(jnp.int32, (rows * heads, LANES), 1)
    for copy in copies[:3]:
        copy.wait()
    scores = [
        lax.dot_general(
            query_ref[row], key_ref[row, 0], (((1,), (1,)), ((), ())),
            preferred_element_type=jnp.float32,
        )
        for row in range(rows)
    ]
    live = jnp.concatenate([positions < lengths_ref[row] for row in range(rows)])
    masked = jnp.where(live, jnp.concatenate(scores) * head_dim ** (-0.5), -1e30)
    top = jnp.max(masked, axis=1, keepdims=True)
    high, low = halves_of(top)
    low = low.astype(jnp.bfloat16).astype(jnp.float32)
    weights = jnp.where(live, jnp.exp(masked - (high + low)), 0.0)
    rounded = weights.astype(jnp.bfloat16)
    copies[3].wait()
    for row in range(rows):
        out_ref[row] = jnp.dot(
            rounded[row * heads : (row + 1) * heads], value_ref[row, 0],
            preferred_element_type=jnp.float32,
        ).astype(jnp.bfloat16)
    total_high, total_low = halves_of(jnp.sum(weights, axis=1, keepdims=True))
    stats = jnp.where(lane == 0, high, jnp.where(lane == 1, low, 0.0))
    stats = jnp.where(lane == 2, total_high, jnp.where(lane == 3, total_low, stats))
    empty = jnp.zeros((LANES - rows * heads, LANES), jnp.float32)
    stats_ref[...] = jnp.concatenate([stats, empty]).T[:8]
    for copy in copies[4:]:
        copy.wait()


def project(blocks_ref, weight_ref, out_ref, attention_ref):
    count = blocks_ref.shape[0]
    pairs = attention_ref.shape[0]
    rows = out_ref.shape[0]
    heads = pairs // rows
    blocks = [blocks_ref[at].astype(jnp.float32) for at in range(count)]
    stats = [block[pairs : pairs + 8] for block in blocks]
    peaks = [stat[0:1] + stat[1:2] for stat in stats]
    peak = peaks[0]
    for other in peaks[1:]:
        peak = jnp.maximum(peak, other)
    factors = [jnp.exp(other - peak) for other in peaks]
    lane = lax.broadcasted_iota(jnp.int32, (1, LANES), 1)
    total = jnp.where(lane < pairs, 0.0, 1.0)
    for factor, stat in zip(factors, stats):
        total = total + factor * (stat[2:3] + stat[3:4])
    factors = jnp.concatenate([factor / total for factor in factors])
    empty = jnp.zeros((LANES - count, LANES), jnp.float32)
    columns = jnp.concatenate([factors, empty]).T
    attention = blocks[0][:pairs] * columns[:pairs, 0:1]
    for at in range(1, count):
        attention = attention + blocks[at][:pairs] * columns[:pairs, at : at + 1]
    attention_ref[...] = attention
    attention = jnp.concatenate(
        [attention_ref[pl.ds(head, rows, stride=heads), :] for head in range(heads)], axis=1
    ).astype(jnp.bfloat16)
    out_ref[...] = jnp.dot(attention, weight_ref[...], preferred_element_type=jnp.float32)


def feed(terms_ref, residual_ref, gain_ref, gate_ref, up_ref, mixed_ref, wide_ref):
    mixed = residual_ref[...].astype(jnp.float32)
    for at in range(terms_ref.shape[0]):
        mixed = mixed + terms_ref[at]
    mixed_ref[...] = mixed
    rows = mixed.shape[0]
    halves = NEAR // rows
    deep = gate_ref.shape[1] // halves // LANES
    squares = jnp.sum(mixed * mixed, axis=1, keepdims=True)
    high, low = halves_of(jnp.broadcast_to(squares, (rows, LANES)))
    wide_ref[...] = jnp.zeros_like(wide_ref)
    for half in range(halves):
        wide_ref[pl.ds(half, rows, stride=halves), 2 * deep, :] = high
        wide_ref[pl.ds(half, rows, stride=halves), 2 * deep + 1, :] = low
    scaled = (mixed * gain_ref[...]).astype(jnp.bfloat16)
    for first, weight_ref in ((0, gate_ref), (deep, up_ref)):
        terms = jnp.dot(scaled, weight_ref[...], preferred_element_type=jnp.float32)
        for half in range(halves):
            for at in range(deep):
                column = (half * deep + at) * LANES
                piece = terms[:, column : column + LANES]
                wide_ref[pl.ds(half, rows, stride=halves), first + at, :] = piece


def finish(mixed_ref, blocks_ref, stream_hbm, hidden_hbm, wide_ref, stream_ref, hidden_ref, sent):
    stream_ref[...] = mixed_ref[...].astype(jnp.bfloat16)
    first = pltpu.make_async_copy(stream_ref, stream_hbm, sent.at[0])
    first.start()
    rows = stream_ref.shape[0]
    halves = NEAR // rows
    deep = blocks_ref.shape[1]
    wide_ref[...] = blocks_ref[...].astype(jnp.float32)
    for half in range(halves):
        for at in range(deep):
            piece = wide_ref[pl.ds(half, rows, stride=halves), at, :]
            column = (half * deep + at) * LANES
            hidden_ref[:, column : column + LANES] = piece.astype(jnp.bfloat16)
    second = pltpu.make_async_copy(hidden_ref, hidden_hbm, sent.at[1])
    second.start()
    first.wait()
    second.wait()


def local(
    query, key_cache, value_cache, lengths, out_weight, residual, norm_gain, gate_weight, up_weight
):
    rows, heads, head_dim = query.shape
    near, far = teams(lax.axis_size("kvp"))
    vmem, hbm = pl.BlockSpec(memory_space=pltpu.VMEM), pl.BlockSpec(memory_space=pltpu.HBM)
    params = pltpu.CompilerParams(vmem_limit_bytes=16 * 2**20)
    sources = (lengths, query, key_cache, value_cache, up_weight)
    out, stats, up_weight = pl.pallas_call(
        attend,
        out_shape=(
            pltpu.VMEM((rows, heads, head_dim), jnp.bfloat16),
            pltpu.VMEM((8, LANES), jnp.float32),
            pltpu.VMEM(up_weight.shape, jnp.bfloat16),
        ),
        in_specs=[hbm] * len(sources),
        out_specs=(vmem,) * 3,
        scratch_shapes=[
            pltpu.SMEM(lengths.shape, jnp.int32),
            pltpu.VMEM(query.shape, jnp.bfloat16),
            pltpu.VMEM(key_cache.shape, jnp.bfloat16),
            pltpu.VMEM(value_cache.shape, jnp.bfloat16),
            pltpu.SemaphoreType.DMA((len(sources),)),
        ],
        compiler_params=params,
    )(*[pltpu.with_memory_space_constraint(source, pltpu.HBM) for source in sources])
    out = out.reshape(rows * heads, head_dim)
    out, peak, total = combine(spread(pack(out, stats), "kvp", near))
    blocks = spread(pack(out, stacked(peak, total)), "kvp", far)
    block_width = out_weight.shape[1]
    projected = pl.pallas_call(
        project,
        out_shape=jax.ShapeDtypeStruct((rows, block_width), jnp.float32),
        in_specs=[vmem] * 2,
        out_specs=vmem,
        scratch_shapes=[pltpu.VMEM((rows * heads, head_dim), jnp.float32)],
        compiler_params=params,
    )(blocks, out_weight)
    width = gate_weight.shape[1]
    halves = NEAR // rows
    deep = width // halves // LANES
    tall = -(-(2 * deep + 2) // 16) * 16
    mixed, terms = pl.pallas_call(
        feed,
        out_shape=(
            pltpu.VMEM((rows, block_width), jnp.float32),
            pltpu.VMEM((NEAR, tall, LANES), jnp.float32),
        ),
        in_specs=[vmem] * 5,
        out_specs=(vmem,) * 2,
        compiler_params=params,
    )(spread(projected, "tp"), residual, norm_gain.reshape(1, -1), gate_weight, up_weight)

    terms = exchange(terms.astype(jnp.bfloat16), "kvp", near)
    terms = jnp.sum(terms.astype(jnp.float32), axis=0)
    pair = jnp.stack(split_pair(terms[2 * deep] + terms[2 * deep + 1]))
    terms = jnp.concatenate([terms[: 2 * deep], pair, terms[2 * deep + 2 :]]).astype(jnp.bfloat16)
    terms = jnp.sum(spread(terms, "kvp", far).astype(jnp.float32), axis=0)
    features = block_width * lax.axis_size("kvp")
    mean_square = (terms[2 * deep] + terms[2 * deep + 1]) / features
    inv_rms = lax.rsqrt(mean_square + 1e-05)
    gate_sum = terms[:deep] * inv_rms
    up_sum = terms[deep : 2 * deep] * inv_rms
    hidden = (jax.nn.silu(gate_sum) * up_sum).astype(jnp.bfloat16)
    blocks = spread(hidden, "kvp", near)
    return tuple(pl.pallas_call(
        finish,
        out_shape=(
            jax.ShapeDtypeStruct((rows, block_width), jnp.bfloat16),
            jax.ShapeDtypeStruct((rows, width), jnp.bfloat16),
        ),
        in_specs=[vmem] * 2,
        out_specs=(hbm, hbm),
        scratch_shapes=[
            pltpu.VMEM(blocks.shape, jnp.float32),
            pltpu.VMEM((rows, block_width), jnp.bfloat16),
            pltpu.VMEM((rows, width), jnp.bfloat16),
            pltpu.SemaphoreType.DMA((2,)),
        ],
        compiler_params=params,
    )(mixed, blocks))


def solution(mesh):
    placed = (
        P(None, "tp", None),
        P(None, "tp", "kvp", None),
        P(None, "tp", "kvp", None),
        P(),
        P("tp", "kvp"),
        P(None, "kvp"),
        P("kvp"),
        P("kvp", "tp"),
        P("kvp", "tp"),
    )
    return jax.shard_map(
        local,
        mesh=mesh,
        in_specs=placed,
        out_specs=(P(None, "kvp"), P(None, "tp")),
        check_vma=False,
    )
```

```python
import jax
import jax.numpy as jnp
from jax import lax
from jax.experimental import pallas as pl
from jax.experimental.pallas import tpu as pltpu
from jax.sharding import PartitionSpec as P

NEAR = 8
LANES = 128
NEAR_LEAD = 6


def led(group, by):
    return group[by:] + group[:by]


def teams(count):
    near = []
    for first in range(0, count, NEAR):
        turn = NEAR // 2 if 2 * first >= count else 0
        near.append(led([first + (at ^ turn) for at in range(NEAR)], NEAR_LEAD))
    return near, [led(list(far), len(far) // 2) for far in zip(*near)]


def exchange(blocks, axis, groups=None):
    return lax.all_to_all(blocks, axis, 0, 0, axis_index_groups=groups, tiled=True)


def spread(block, axis, groups=None):
    count = len(groups[0]) if groups else lax.axis_size(axis)
    return exchange(jnp.broadcast_to(block[None], (count,) + block.shape), axis, groups)


def split_pair(value):
    high = lax.reduce_precision(value, 8, 7)
    low = lax.reduce_precision(value - high, 8, 7)
    return high, low


def pack(out, stats):
    return jnp.concatenate([out.astype(jnp.bfloat16), stats.astype(jnp.bfloat16)])


def combine(blocks):
    pairs = blocks.shape[1] - 8
    out = blocks[:, :pairs].astype(jnp.float32)
    stats = blocks[:, pairs:, :pairs].astype(jnp.float32)
    peaks = stats[:, 0] + stats[:, 1]
    totals = stats[:, 2] + stats[:, 3]
    peak = jnp.max(peaks, axis=0)
    factor = jnp.exp(peaks - peak[None])
    total = jnp.sum(totals * factor, axis=0)
    return jnp.sum(out * factor[..., None], axis=0), peak, total


def stacked(peak, total):
    stats = jnp.stack(split_pair(peak) + split_pair(total))
    return jnp.pad(stats, ((0, 4), (0, LANES - stats.shape[1])))


def halves_of(value):
    high = value.astype(jnp.bfloat16).astype(jnp.float32)
    return high, value - high


def attend(
    lengths_hbm, query_hbm, key_hbm, value_hbm, *others,
):
    count = (len(others) - 7) // 2
    out_ref, stats_ref, *fetched = others[count : 2 * count + 2]
    lengths_ref, query_ref, key_ref, value_ref, arrived = others[2 * count + 2 :]
    sources = (lengths_hbm, query_hbm, key_hbm, value_hbm, *others[:count])
    targets = (lengths_ref, query_ref, key_ref, value_ref, *fetched)
    copies = [
        pltpu.make_async_copy(source, target, arrived.at[at])
        for at, (source, target) in enumerate(zip(sources, targets))
    ]
    for copy in copies:
        copy.start()
    rows, heads, head_dim = query_ref.shape
    span = key_ref.shape[2]
    block = lax.axis_index("kvp")
    positions = block * span + lax.broadcasted_iota(jnp.int32, (heads, span), 1)
    lane = lax.broadcasted_iota(jnp.int32, (rows * heads, LANES), 1)
    for copy in copies[:3]:
        copy.wait()
    scores = [
        lax.dot_general(
            query_ref[row], key_ref[row, 0], (((1,), (1,)), ((), ())),
            preferred_element_type=jnp.float32,
        )
        for row in range(rows)
    ]
    live = jnp.concatenate([positions < lengths_ref[row] for row in range(rows)])
    masked = jnp.where(live, jnp.concatenate(scores) * head_dim ** (-0.5), -1e30)
    top = jnp.max(masked, axis=1, keepdims=True)
    high, low = halves_of(top)
    low = low.astype(jnp.bfloat16).astype(jnp.float32)
    weights = jnp.where(live, jnp.exp(masked - (high + low)), 0.0)
    rounded = weights.astype(jnp.bfloat16)
    copies[3].wait()
    for row in range(rows):
        out_ref[row] = jnp.dot(
            rounded[row * heads : (row + 1) * heads], value_ref[row, 0],
            preferred_element_type=jnp.float32,
        ).astype(jnp.bfloat16)
    total_high, total_low = halves_of(jnp.sum(weights, axis=1, keepdims=True))
    stats = jnp.where(lane == 0, high, jnp.where(lane == 1, low, 0.0))
    stats = jnp.where(lane == 2, total_high, jnp.where(lane == 3, total_low, stats))
    empty = jnp.zeros((LANES - rows * heads, LANES), jnp.float32)
    stats_ref[...] = jnp.concatenate([stats, empty]).T[:8]
    for copy in copies[4:]:
        copy.wait()


def project(blocks_ref, weight_ref, out_ref, attention_ref):
    count = blocks_ref.shape[0]
    pairs = attention_ref.shape[0]
    rows = out_ref.shape[0]
    heads = pairs // rows
    blocks = [blocks_ref[at].astype(jnp.float32) for at in range(count)]
    stats = [block[pairs : pairs + 8] for block in blocks]
    peaks = [stat[0:1] + stat[1:2] for stat in stats]
    peak = peaks[0]
    for other in peaks[1:]:
        peak = jnp.maximum(peak, other)
    factors = [jnp.exp(other - peak) for other in peaks]
    lane = lax.broadcasted_iota(jnp.int32, (1, LANES), 1)
    total = jnp.where(lane < pairs, 0.0, 1.0)
    for factor, stat in zip(factors, stats):
        total = total + factor * (stat[2:3] + stat[3:4])
    factors = jnp.concatenate([factor / total for factor in factors])
    empty = jnp.zeros((LANES - count, LANES), jnp.float32)
    columns = jnp.concatenate([factors, empty]).T
    attention = blocks[0][:pairs] * columns[:pairs, 0:1]
    for at in range(1, count):
        attention = attention + blocks[at][:pairs] * columns[:pairs, at : at + 1]
    attention_ref[...] = attention
    attention = jnp.concatenate(
        [attention_ref[pl.ds(head, rows, stride=heads), :] for head in range(heads)], axis=1
    ).astype(jnp.bfloat16)
    out_ref[...] = jnp.dot(attention, weight_ref[...], preferred_element_type=jnp.float32)


def feed(terms_ref, residual_ref, gain_ref, gate_ref, up_ref, mixed_ref, wide_ref):
    mixed = residual_ref[...].astype(jnp.float32)
    for at in range(terms_ref.shape[0]):
        mixed = mixed + terms_ref[at]
    mixed_ref[...] = mixed
    rows = mixed.shape[0]
    halves = NEAR // rows
    deep = gate_ref.shape[1] // halves // LANES
    squares = jnp.sum(mixed * mixed, axis=1, keepdims=True)
    high, low = halves_of(jnp.broadcast_to(squares, (rows, LANES)))
    wide_ref[...] = jnp.zeros_like(wide_ref)
    for half in range(halves):
        wide_ref[pl.ds(half, rows, stride=halves), 2 * deep, :] = high
        wide_ref[pl.ds(half, rows, stride=halves), 2 * deep + 1, :] = low
    scaled = (mixed * gain_ref[...]).astype(jnp.bfloat16)
    for first, weight_ref in ((0, gate_ref), (deep, up_ref)):
        terms = jnp.dot(scaled, weight_ref[...], preferred_element_type=jnp.float32)
        for half in range(halves):
            for at in range(deep):
                column = (half * deep + at) * LANES
                piece = terms[:, column : column + LANES]
                wide_ref[pl.ds(half, rows, stride=halves), first + at, :] = piece


def finish(mixed_ref, blocks_ref, stream_hbm, hidden_hbm, wide_ref, stream_ref, hidden_ref, sent):
    stream_ref[...] = mixed_ref[...].astype(jnp.bfloat16)
    first = pltpu.make_async_copy(stream_ref, stream_hbm, sent.at[0])
    first.start()
    rows = stream_ref.shape[0]
    halves = NEAR // rows
    deep = blocks_ref.shape[1]
    wide_ref[...] = blocks_ref[...].astype(jnp.float32)
    for half in range(halves):
        for at in range(deep):
            piece = wide_ref[pl.ds(half, rows, stride=halves), at, :]
            column = (half * deep + at) * LANES
            hidden_ref[:, column : column + LANES] = piece.astype(jnp.bfloat16)
    second = pltpu.make_async_copy(hidden_ref, hidden_hbm, sent.at[1])
    second.start()
    first.wait()
    second.wait()


def local(
    query, key_cache, value_cache, lengths, out_weight, residual, norm_gain, gate_weight, up_weight
):
    rows, heads, head_dim = query.shape
    near, far = teams(lax.axis_size("kvp"))
    tp = lax.axis_size("tp")
    vmem, hbm = pl.BlockSpec(memory_space=pltpu.VMEM), pl.BlockSpec(memory_space=pltpu.HBM)
    params = pltpu.CompilerParams(vmem_limit_bytes=16 * 2**20)
    sources = (lengths, query, key_cache, value_cache, up_weight)
    out, stats, up_weight = pl.pallas_call(
        attend,
        out_shape=(
            pltpu.VMEM((rows, heads, head_dim), jnp.bfloat16),
            pltpu.VMEM((8, LANES), jnp.float32),
            pltpu.VMEM(up_weight.shape, jnp.bfloat16),
        ),
        in_specs=[hbm] * len(sources),
        out_specs=(vmem,) * 3,
        scratch_shapes=[
            pltpu.SMEM(lengths.shape, jnp.int32),
            pltpu.VMEM(query.shape, jnp.bfloat16),
            pltpu.VMEM(key_cache.shape, jnp.bfloat16),
            pltpu.VMEM(value_cache.shape, jnp.bfloat16),
            pltpu.SemaphoreType.DMA((len(sources),)),
        ],
        compiler_params=params,
    )(*[pltpu.with_memory_space_constraint(source, pltpu.HBM) for source in sources])
    out = out.reshape(rows * heads, head_dim)
    out, peak, total = combine(spread(pack(out, stats), "kvp", near))
    blocks = spread(pack(out, stacked(peak, total)), "kvp", far)
    block_width = out_weight.shape[1]
    projected = pl.pallas_call(
        project,
        out_shape=jax.ShapeDtypeStruct((rows, block_width), jnp.float32),
        in_specs=[vmem] * 2,
        out_specs=vmem,
        scratch_shapes=[pltpu.VMEM((rows * heads, head_dim), jnp.float32)],
        compiler_params=params,
    )(blocks, out_weight)
    width = gate_weight.shape[1]
    halves = NEAR // rows
    deep = width // halves // LANES
    tall = -(-(2 * deep + 2) // 16) * 16
    mixed, terms = pl.pallas_call(
        feed,
        out_shape=(
            pltpu.VMEM((rows, block_width), jnp.float32),
            pltpu.VMEM((NEAR, tall, LANES), jnp.float32),
        ),
        in_specs=[vmem] * 5,
        out_specs=(vmem,) * 2,
        compiler_params=params,
    )(spread(projected, "tp", [led(list(range(tp)), (tp // 2 + 1) % tp)]), residual, norm_gain.reshape(1, -1), gate_weight, up_weight)

    terms = exchange(terms.astype(jnp.bfloat16), "kvp", near)
    terms = jnp.sum(terms.astype(jnp.float32), axis=0)
    pair = jnp.stack(split_pair(terms[2 * deep] + terms[2 * deep + 1]))
    terms = jnp.concatenate([terms[: 2 * deep], pair, terms[2 * deep + 2 :]]).astype(jnp.bfloat16)
    terms = jnp.sum(spread(terms, "kvp", far).astype(jnp.float32), axis=0)
    features = block_width * lax.axis_size("kvp")
    mean_square = (terms[2 * deep] + terms[2 * deep + 1]) / features
    inv_rms = lax.rsqrt(mean_square + 1e-05)
    gate_sum = terms[:deep] * inv_rms
    up_sum = terms[deep : 2 * deep] * inv_rms
    hidden = (jax.nn.silu(gate_sum) * up_sum).astype(jnp.bfloat16)
    blocks = spread(hidden, "kvp", near)
    return tuple(pl.pallas_call(
        finish,
        out_shape=(
            jax.ShapeDtypeStruct((rows, block_width), jnp.bfloat16),
            jax.ShapeDtypeStruct((rows, width), jnp.bfloat16),
        ),
        in_specs=[vmem] * 2,
        out_specs=(hbm, hbm),
        scratch_shapes=[
            pltpu.VMEM(blocks.shape, jnp.float32),
            pltpu.VMEM((rows, block_width), jnp.bfloat16),
            pltpu.VMEM((rows, width), jnp.bfloat16),
            pltpu.SemaphoreType.DMA((2,)),
        ],
        compiler_params=params,
    )(mixed, blocks))


def solution(mesh):
    placed = (
        P(None, "tp", None),
        P(None, "tp", "kvp", None),
        P(None, "tp", "kvp", None),
        P(),
        P("tp", "kvp"),
        P(None, "kvp"),
        P("kvp"),
        P("kvp", "tp"),
        P("kvp", "tp"),
    )
    return jax.shard_map(
        local,
        mesh=mesh,
        in_specs=placed,
        out_specs=(P(None, "kvp"), P(None, "tp")),
        check_vma=False,
    )
```

```python
import jax
import jax.numpy as jnp
from jax import lax
from jax.experimental import pallas as pl
from jax.experimental.pallas import tpu as pltpu
from jax.sharding import PartitionSpec as P

NEAR = 8
LANES = 128
TURN = NEAR // 2
NEAR_LEAD = 6


def led(group, by):
    return group[by:] + group[:by]


def teams(count):
    near = []
    for first in range(0, count, NEAR):
        turn = NEAR // 2 if 2 * first >= count else 0
        near.append(led([first + (at ^ turn) for at in range(NEAR)], NEAR_LEAD))
    return near, [led(list(far), count // NEAR // 2) for far in zip(*near)]


def exchange(blocks, axis, groups=None):
    return lax.all_to_all(blocks, axis, 0, 0, axis_index_groups=groups, tiled=True)


def spread(block, axis, groups=None):
    count = len(groups[0]) if groups else lax.axis_size(axis)
    return exchange(jnp.broadcast_to(block[None], (count,) + block.shape), axis, groups)


def split_pair(value):
    high = lax.reduce_precision(value, 8, 7)
    low = lax.reduce_precision(value - high, 8, 7)
    return high, low


def pack(out, stats):
    return jnp.concatenate([out.astype(jnp.bfloat16), stats.astype(jnp.bfloat16)])


def combine(blocks):
    pairs = blocks.shape[1] - 8
    out = blocks[:, :pairs].astype(jnp.float32)
    stats = blocks[:, pairs:, :pairs].astype(jnp.float32)
    peaks = stats[:, 0] + stats[:, 1]
    totals = stats[:, 2] + stats[:, 3]
    peak = jnp.max(peaks, axis=0)
    factor = jnp.exp(peaks - peak[None])
    total = jnp.sum(totals * factor, axis=0)
    return jnp.sum(out * factor[..., None], axis=0), peak, total


def stacked(peak, total):
    stats = jnp.stack(split_pair(peak) + split_pair(total))
    return jnp.pad(stats, ((0, 4), (0, LANES - stats.shape[1])))


def halves_of(value):
    high = value.astype(jnp.bfloat16).astype(jnp.float32)
    return high, value - high


def attend(
    lengths_hbm, query_hbm, key_hbm, value_hbm, *others,
):
    count = (len(others) - 7) // 2
    out_ref, stats_ref, *fetched = others[count : 2 * count + 2]
    lengths_ref, query_ref, key_ref, value_ref, arrived = others[2 * count + 2 :]
    sources = (lengths_hbm, query_hbm, key_hbm, value_hbm, *others[:count])
    targets = (lengths_ref, query_ref, key_ref, value_ref, *fetched)
    copies = [
        pltpu.make_async_copy(source, target, arrived.at[at])
        for at, (source, target) in enumerate(zip(sources, targets))
    ]
    for copy in copies:
        copy.start()
    rows, heads, head_dim = query_ref.shape
    span = key_ref.shape[2]
    block = lax.axis_index("kvp")
    positions = block * span + lax.broadcasted_iota(jnp.int32, (heads, span), 1)
    lane = lax.broadcasted_iota(jnp.int32, (rows * heads, LANES), 1)
    for copy in copies[:3]:
        copy.wait()
    scores = [
        lax.dot_general(
            query_ref[row], key_ref[row, 0], (((1,), (1,)), ((), ())),
            preferred_element_type=jnp.float32,
        )
        for row in range(rows)
    ]
    live = jnp.concatenate([positions < lengths_ref[row] for row in range(rows)])
    masked = jnp.where(live, jnp.concatenate(scores) * head_dim ** (-0.5), -1e30)
    top = jnp.max(masked, axis=1, keepdims=True)
    high, low = halves_of(top)
    low = low.astype(jnp.bfloat16).astype(jnp.float32)
    weights = jnp.where(live, jnp.exp(masked - (high + low)), 0.0)
    rounded = weights.astype(jnp.bfloat16)
    copies[3].wait()
    for row in range(rows):
        out_ref[row] = jnp.dot(
            rounded[row * heads : (row + 1) * heads], value_ref[row, 0],
            preferred_element_type=jnp.float32,
        ).astype(jnp.bfloat16)
    total_high, total_low = halves_of(jnp.sum(weights, axis=1, keepdims=True))
    stats = jnp.where(lane == 0, high, jnp.where(lane == 1, low, 0.0))
    stats = jnp.where(lane == 2, total_high, jnp.where(lane == 3, total_low, stats))
    empty = jnp.zeros((LANES - rows * heads, LANES), jnp.float32)
    stats_ref[...] = jnp.concatenate([stats, empty]).T[:8]
    for copy in copies[4:]:
        copy.wait()


def project(blocks_ref, weight_ref, out_ref, attention_ref):
    count = blocks_ref.shape[0]
    pairs = attention_ref.shape[0]
    rows = out_ref.shape[0]
    heads = pairs // rows
    blocks = [blocks_ref[at].astype(jnp.float32) for at in range(count)]
    stats = [block[pairs : pairs + 8] for block in blocks]
    peaks = [stat[0:1] + stat[1:2] for stat in stats]
    peak = peaks[0]
    for other in peaks[1:]:
        peak = jnp.maximum(peak, other)
    factors = [jnp.exp(other - peak) for other in peaks]
    lane = lax.broadcasted_iota(jnp.int32, (1, LANES), 1)
    total = jnp.where(lane < pairs, 0.0, 1.0)
    for factor, stat in zip(factors, stats):
        total = total + factor * (stat[2:3] + stat[3:4])
    factors = jnp.concatenate([factor / total for factor in factors])
    empty = jnp.zeros((LANES - count, LANES), jnp.float32)
    columns = jnp.concatenate([factors, empty]).T
    attention = blocks[0][:pairs] * columns[:pairs, 0:1]
    for at in range(1, count):
        attention = attention + blocks[at][:pairs] * columns[:pairs, at : at + 1]
    attention_ref[...] = attention
    attention = jnp.concatenate(
        [attention_ref[pl.ds(head, rows, stride=heads), :] for head in range(heads)], axis=1
    ).astype(jnp.bfloat16)
    out_ref[...] = jnp.dot(attention, weight_ref[...], preferred_element_type=jnp.float32)


def feed(terms_ref, residual_ref, gain_ref, gate_ref, up_ref, mixed_ref, wide_ref):
    mixed = residual_ref[...].astype(jnp.float32)
    for at in range(terms_ref.shape[0]):
        mixed = mixed + terms_ref[at]
    mixed_ref[...] = mixed
    rows = mixed.shape[0]
    halves = NEAR // rows
    deep = gate_ref.shape[1] // halves // LANES
    squares = jnp.sum(mixed * mixed, axis=1, keepdims=True)
    high, low = halves_of(jnp.broadcast_to(squares, (rows, LANES)))
    wide_ref[...] = jnp.zeros_like(wide_ref)
    for half in range(halves):
        wide_ref[pl.ds(half, rows, stride=halves), 2 * deep, :] = high
        wide_ref[pl.ds(half, rows, stride=halves), 2 * deep + 1, :] = low
    scaled = (mixed * gain_ref[...]).astype(jnp.bfloat16)
    for first, weight_ref in ((0, gate_ref), (deep, up_ref)):
        terms = jnp.dot(scaled, weight_ref[...], preferred_element_type=jnp.float32)
        for half in range(halves):
            for at in range(deep):
                column = (half * deep + at) * LANES
                piece = terms[:, column : column + LANES]
                wide_ref[pl.ds(half, rows, stride=halves), first + at, :] = piece


def finish(mixed_ref, blocks_ref, stream_hbm, hidden_hbm, wide_ref, stream_ref, hidden_ref, sent):
    stream_ref[...] = mixed_ref[...].astype(jnp.bfloat16)
    first = pltpu.make_async_copy(stream_ref, stream_hbm, sent.at[0])
    first.start()
    rows = stream_ref.shape[0]
    halves = NEAR // rows
    deep = blocks_ref.shape[1]
    wide_ref[:TURN] = blocks_ref[TURN:].astype(jnp.float32)
    wide_ref[TURN:] = blocks_ref[:TURN].astype(jnp.float32)
    for half in range(halves):
        for at in range(deep):
            piece = wide_ref[pl.ds(half, rows, stride=halves), at, :]
            column = (half * deep + at) * LANES
            hidden_ref[:, column : column + LANES] = piece.astype(jnp.bfloat16)
    second = pltpu.make_async_copy(hidden_ref, hidden_hbm, sent.at[1])
    second.start()
    first.wait()
    second.wait()


def local(
    query, key_cache, value_cache, lengths, out_weight, residual, norm_gain, gate_weight, up_weight
):
    rows, heads, head_dim = query.shape
    near, far = teams(lax.axis_size("kvp"))
    tp = lax.axis_size("tp")
    vmem, hbm = pl.BlockSpec(memory_space=pltpu.VMEM), pl.BlockSpec(memory_space=pltpu.HBM)
    params = pltpu.CompilerParams(vmem_limit_bytes=16 * 2**20)
    sources = (lengths, query, key_cache, value_cache, up_weight)
    out, stats, up_weight = pl.pallas_call(
        attend,
        out_shape=(
            pltpu.VMEM((rows, heads, head_dim), jnp.bfloat16),
            pltpu.VMEM((8, LANES), jnp.float32),
            pltpu.VMEM(up_weight.shape, jnp.bfloat16),
        ),
        in_specs=[hbm] * len(sources),
        out_specs=(vmem,) * 3,
        scratch_shapes=[
            pltpu.SMEM(lengths.shape, jnp.int32),
            pltpu.VMEM(query.shape, jnp.bfloat16),
            pltpu.VMEM(key_cache.shape, jnp.bfloat16),
            pltpu.VMEM(value_cache.shape, jnp.bfloat16),
            pltpu.SemaphoreType.DMA((len(sources),)),
        ],
        compiler_params=params,
    )(*[pltpu.with_memory_space_constraint(source, pltpu.HBM) for source in sources])
    out = out.reshape(rows * heads, head_dim)
    out, peak, total = combine(spread(pack(out, stats), "kvp", near))
    blocks = spread(pack(out, stacked(peak, total)), "kvp", [led(team, 1) for team in far])
    block_width = out_weight.shape[1]
    projected = pl.pallas_call(
        project,
        out_shape=jax.ShapeDtypeStruct((rows, block_width), jnp.float32),
        in_specs=[vmem] * 2,
        out_specs=vmem,
        scratch_shapes=[pltpu.VMEM((rows * heads, head_dim), jnp.float32)],
        compiler_params=params,
    )(blocks, out_weight)
    width = gate_weight.shape[1]
    halves = NEAR // rows
    deep = width // halves // LANES
    tall = -(-(2 * deep + 2) // 16) * 16
    mixed, terms = pl.pallas_call(
        feed,
        out_shape=(
            pltpu.VMEM((rows, block_width), jnp.float32),
            pltpu.VMEM((NEAR, tall, LANES), jnp.float32),
        ),
        in_specs=[vmem] * 5,
        out_specs=(vmem,) * 2,
        compiler_params=params,
    )(spread(projected, "tp", [led(list(range(tp)), (tp // 2 + 1) % tp)]), residual, norm_gain.reshape(1, -1), gate_weight, up_weight)

    terms = exchange(terms.astype(jnp.bfloat16), "kvp", [led(team, TURN) for team in near])
    terms = jnp.sum(terms.astype(jnp.float32), axis=0)
    pair = jnp.stack(split_pair(terms[2 * deep] + terms[2 * deep + 1]))
    terms = jnp.concatenate([terms[: 2 * deep], pair, terms[2 * deep + 2 :]]).astype(jnp.bfloat16)
    terms = jnp.sum(spread(terms, "kvp", far).astype(jnp.float32), axis=0)
    features = block_width * lax.axis_size("kvp")
    mean_square = (terms[2 * deep] + terms[2 * deep + 1]) / features
    inv_rms = lax.rsqrt(mean_square + 1e-05)
    gate_sum = terms[:deep] * inv_rms
    up_sum = terms[deep : 2 * deep] * inv_rms
    hidden = (jax.nn.silu(gate_sum) * up_sum).astype(jnp.bfloat16)
    blocks = spread(hidden, "kvp", near)
    return tuple(pl.pallas_call(
        finish,
        out_shape=(
            jax.ShapeDtypeStruct((rows, block_width), jnp.bfloat16),
            jax.ShapeDtypeStruct((rows, width), jnp.bfloat16),
        ),
        in_specs=[vmem] * 2,
        out_specs=(hbm, hbm),
        scratch_shapes=[
            pltpu.VMEM(blocks.shape, jnp.float32),
            pltpu.VMEM((rows, block_width), jnp.bfloat16),
            pltpu.VMEM((rows, width), jnp.bfloat16),
            pltpu.SemaphoreType.DMA((2,)),
        ],
        compiler_params=params,
    )(mixed, blocks))


def solution(mesh):
    placed = (
        P(None, "tp", None),
        P(None, "tp", "kvp", None),
        P(None, "tp", "kvp", None),
        P(),
        P("tp", "kvp"),
        P(None, "kvp"),
        P("kvp"),
        P("kvp", "tp"),
        P("kvp", "tp"),
    )
    return jax.shard_map(
        local,
        mesh=mesh,
        in_specs=placed,
        out_specs=(P(None, "kvp"), P(None, "tp")),
        check_vma=False,
    )
```

```python
import jax
import jax.numpy as jnp
from jax import lax
from jax.experimental import pallas as pl
from jax.experimental.pallas import tpu as pltpu
from jax.sharding import PartitionSpec as P

NEAR = 8
LANES = 128
TURN = NEAR // 2
NEAR_LEAD = 6


def led(group, by):
    return group[by:] + group[:by]


def teams(count):
    near = []
    for first in range(0, count, NEAR):
        turn = NEAR // 2 if 2 * first >= count else 0
        near.append(led([first + (at ^ turn) for at in range(NEAR)], NEAR_LEAD))
    return near, [led(list(far), count // NEAR // 2) for far in zip(*near)]


def exchange(blocks, axis, groups=None):
    return lax.all_to_all(blocks, axis, 0, 0, axis_index_groups=groups, tiled=True)


def spread(block, axis, groups=None):
    count = len(groups[0]) if groups else lax.axis_size(axis)
    return exchange(jnp.broadcast_to(block[None], (count,) + block.shape), axis, groups)


def split_pair(value):
    high = lax.reduce_precision(value, 8, 7)
    low = lax.reduce_precision(value - high, 8, 7)
    return high, low


def pack(out, stats):
    return jnp.concatenate([out.astype(jnp.bfloat16), stats.astype(jnp.bfloat16)])


def combine(blocks):
    pairs = blocks.shape[1] - 8
    out = blocks[:, :pairs].astype(jnp.float32)
    stats = blocks[:, pairs:, :pairs].astype(jnp.float32)
    peaks = stats[:, 0] + stats[:, 1]
    totals = stats[:, 2] + stats[:, 3]
    peak = jnp.max(peaks, axis=0)
    factor = jnp.exp(peaks - peak[None])
    total = jnp.sum(totals * factor, axis=0)
    return jnp.sum(out * factor[..., None], axis=0), peak, total


def stacked(peak, total):
    stats = jnp.stack(split_pair(peak) + split_pair(total))
    return jnp.pad(stats, ((0, 4), (0, LANES - stats.shape[1])))


def halves_of(value):
    high = value.astype(jnp.bfloat16).astype(jnp.float32)
    return high, value - high


def attend(
    lengths_hbm, query_hbm, key_hbm, value_hbm, *others,
):
    count = (len(others) - 7) // 2
    out_ref, stats_ref, *fetched = others[count : 2 * count + 2]
    lengths_ref, query_ref, key_ref, value_ref, arrived = others[2 * count + 2 :]
    sources = (lengths_hbm, query_hbm, key_hbm, value_hbm, *others[:count])
    targets = (lengths_ref, query_ref, key_ref, value_ref, *fetched)
    copies = [
        pltpu.make_async_copy(source, target, arrived.at[at])
        for at, (source, target) in enumerate(zip(sources, targets))
    ]
    for copy in copies:
        copy.start()
    rows, heads, head_dim = query_ref.shape
    span = key_ref.shape[2]
    block = lax.axis_index("kvp")
    positions = block * span + lax.broadcasted_iota(jnp.int32, (heads, span), 1)
    lane = lax.broadcasted_iota(jnp.int32, (rows * heads, LANES), 1)
    for copy in copies[:3]:
        copy.wait()
    scores = [
        lax.dot_general(
            query_ref[row], key_ref[row, 0], (((1,), (1,)), ((), ())),
            preferred_element_type=jnp.float32,
        )
        for row in range(rows)
    ]
    live = jnp.concatenate([positions < lengths_ref[row] for row in range(rows)])
    masked = jnp.where(live, jnp.concatenate(scores) * head_dim ** (-0.5), -1e30)
    top = jnp.max(masked, axis=1, keepdims=True)
    high, low = halves_of(top)
    low = low.astype(jnp.bfloat16).astype(jnp.float32)
    weights = jnp.where(live, jnp.exp(masked - (high + low)), 0.0)
    rounded = weights.astype(jnp.bfloat16)
    copies[3].wait()
    for row in range(rows):
        out_ref[row] = jnp.dot(
            rounded[row * heads : (row + 1) * heads], value_ref[row, 0],
            preferred_element_type=jnp.float32,
        ).astype(jnp.bfloat16)
    total_high, total_low = halves_of(jnp.sum(weights, axis=1, keepdims=True))
    stats = jnp.where(lane == 0, high, jnp.where(lane == 1, low, 0.0))
    stats = jnp.where(lane == 2, total_high, jnp.where(lane == 3, total_low, stats))
    empty = jnp.zeros((LANES - rows * heads, LANES), jnp.float32)
    stats_ref[...] = jnp.concatenate([stats, empty]).T[:8]
    for copy in copies[4:]:
        copy.wait()


def project(blocks_ref, weight_ref, out_ref, attention_ref):
    count = blocks_ref.shape[0]
    pairs = attention_ref.shape[0]
    rows = out_ref.shape[0]
    heads = pairs // rows
    blocks = [blocks_ref[at].astype(jnp.float32) for at in range(count)]
    stats = [block[pairs : pairs + 8] for block in blocks]
    peaks = [stat[0:1] + stat[1:2] for stat in stats]
    peak = peaks[0]
    for other in peaks[1:]:
        peak = jnp.maximum(peak, other)
    factors = [jnp.exp(other - peak) for other in peaks]
    lane = lax.broadcasted_iota(jnp.int32, (1, LANES), 1)
    total = jnp.where(lane < pairs, 0.0, 1.0)
    for factor, stat in zip(factors, stats):
        total = total + factor * (stat[2:3] + stat[3:4])
    factors = jnp.concatenate([factor / total for factor in factors])
    empty = jnp.zeros((LANES - count, LANES), jnp.float32)
    columns = jnp.concatenate([factors, empty]).T
    attention = blocks[0][:pairs] * columns[:pairs, 0:1]
    for at in range(1, count):
        attention = attention + blocks[at][:pairs] * columns[:pairs, at : at + 1]
    attention_ref[...] = attention
    attention = jnp.concatenate(
        [attention_ref[pl.ds(head, rows, stride=heads), :] for head in range(heads)], axis=1
    ).astype(jnp.bfloat16)
    out_ref[...] = jnp.dot(attention, weight_ref[...], preferred_element_type=jnp.float32)


def feed(terms_ref, residual_ref, gain_ref, gate_ref, up_ref, mixed_ref, wide_ref):
    mixed = residual_ref[...].astype(jnp.float32)
    for at in range(terms_ref.shape[0]):
        mixed = mixed + terms_ref[at]
    mixed_ref[...] = mixed
    rows = mixed.shape[0]
    halves = NEAR // rows
    deep = gate_ref.shape[1] // halves // LANES
    squares = jnp.sum(mixed * mixed, axis=1, keepdims=True)
    high, low = halves_of(jnp.broadcast_to(squares, (rows, LANES)))
    wide_ref[...] = jnp.zeros_like(wide_ref)
    for half in range(halves):
        wide_ref[pl.ds(half, rows, stride=halves), 2 * deep, :] = high
        wide_ref[pl.ds(half, rows, stride=halves), 2 * deep + 1, :] = low
    scaled = (mixed * gain_ref[...]).astype(jnp.bfloat16)
    for first, weight_ref in ((0, gate_ref), (deep, up_ref)):
        terms = jnp.dot(scaled, weight_ref[...], preferred_element_type=jnp.float32)
        for half in range(halves):
            for at in range(deep):
                column = (half * deep + at) * LANES
                piece = terms[:, column : column + LANES]
                wide_ref[pl.ds(half, rows, stride=halves), first + at, :] = piece


def finish(mixed_ref, blocks_ref, stream_hbm, hidden_hbm, wide_ref, stream_ref, hidden_ref, sent):
    stream_ref[...] = mixed_ref[...].astype(jnp.bfloat16)
    first = pltpu.make_async_copy(stream_ref, stream_hbm, sent.at[0])
    first.start()
    rows = stream_ref.shape[0]
    halves = NEAR // rows
    deep = blocks_ref.shape[1]
    wide_ref[:TURN] = blocks_ref[TURN:].astype(jnp.float32)
    wide_ref[TURN:] = blocks_ref[:TURN].astype(jnp.float32)
    for half in range(halves):
        for at in range(deep):
            piece = wide_ref[pl.ds(half, rows, stride=halves), at, :]
            column = (half * deep + at) * LANES
            hidden_ref[:, column : column + LANES] = piece.astype(jnp.bfloat16)
    second = pltpu.make_async_copy(hidden_ref, hidden_hbm, sent.at[1])
    second.start()
    first.wait()
    second.wait()


def local(
    query, key_cache, value_cache, lengths, out_weight, residual, norm_gain, gate_weight, up_weight
):
    rows, heads, head_dim = query.shape
    near, far = teams(lax.axis_size("kvp"))
    tp = lax.axis_size("tp")
    vmem, hbm = pl.BlockSpec(memory_space=pltpu.VMEM), pl.BlockSpec(memory_space=pltpu.HBM)
    params = pltpu.CompilerParams(vmem_limit_bytes=16 * 2**20)
    sources = (lengths, query, key_cache, value_cache, up_weight)
    out, stats, up_weight = pl.pallas_call(
        attend,
        out_shape=(
            pltpu.VMEM((rows, heads, head_dim), jnp.bfloat16),
            pltpu.VMEM((8, LANES), jnp.float32),
            pltpu.VMEM(up_weight.shape, jnp.bfloat16),
        ),
        in_specs=[hbm] * len(sources),
        out_specs=(vmem,) * 3,
        scratch_shapes=[
            pltpu.SMEM(lengths.shape, jnp.int32),
            pltpu.VMEM(query.shape, jnp.bfloat16),
            pltpu.VMEM(key_cache.shape, jnp.bfloat16),
            pltpu.VMEM(value_cache.shape, jnp.bfloat16),
            pltpu.SemaphoreType.DMA((len(sources),)),
        ],
        compiler_params=params,
    )(*[pltpu.with_memory_space_constraint(source, pltpu.HBM) for source in sources])
    out = out.reshape(rows * heads, head_dim)
    out, peak, total = combine(spread(pack(out, stats), "kvp", [led(team, TURN) for team in near]))
    blocks = spread(pack(out, stacked(peak, total)), "kvp", [led(team, 1) for team in far])
    block_width = out_weight.shape[1]
    projected = pl.pallas_call(
        project,
        out_shape=jax.ShapeDtypeStruct((rows, block_width), jnp.float32),
        in_specs=[vmem] * 2,
        out_specs=vmem,
        scratch_shapes=[pltpu.VMEM((rows * heads, head_dim), jnp.float32)],
        compiler_params=params,
    )(blocks, out_weight)
    width = gate_weight.shape[1]
    halves = NEAR // rows
    deep = width // halves // LANES
    tall = -(-(2 * deep + 2) // 16) * 16
    mixed, terms = pl.pallas_call(
        feed,
        out_shape=(
            pltpu.VMEM((rows, block_width), jnp.float32),
            pltpu.VMEM((NEAR, tall, LANES), jnp.float32),
        ),
        in_specs=[vmem] * 5,
        out_specs=(vmem,) * 2,
        compiler_params=params,
    )(spread(projected, "tp", [led(list(range(tp)), (tp // 2 + 1) % tp)]), residual, norm_gain.reshape(1, -1), gate_weight, up_weight)

    terms = exchange(terms.astype(jnp.bfloat16), "kvp", [led(team, TURN) for team in near])
    terms = jnp.sum(terms.astype(jnp.float32), axis=0)
    pair = jnp.stack(split_pair(terms[2 * deep] + terms[2 * deep + 1]))
    terms = jnp.concatenate([terms[: 2 * deep], pair, terms[2 * deep + 2 :]]).astype(jnp.bfloat16)
    terms = jnp.sum(spread(terms, "kvp", far).astype(jnp.float32), axis=0)
    features = block_width * lax.axis_size("kvp")
    mean_square = (terms[2 * deep] + terms[2 * deep + 1]) / features
    inv_rms = lax.rsqrt(mean_square + 1e-05)
    gate_sum = terms[:deep] * inv_rms
    up_sum = terms[deep : 2 * deep] * inv_rms
    hidden = (jax.nn.silu(gate_sum) * up_sum).astype(jnp.bfloat16)
    blocks = spread(hidden, "kvp", near)
    return tuple(pl.pallas_call(
        finish,
        out_shape=(
            jax.ShapeDtypeStruct((rows, block_width), jnp.bfloat16),
            jax.ShapeDtypeStruct((rows, width), jnp.bfloat16),
        ),
        in_specs=[vmem] * 2,
        out_specs=(hbm, hbm),
        scratch_shapes=[
            pltpu.VMEM(blocks.shape, jnp.float32),
            pltpu.VMEM((rows, block_width), jnp.bfloat16),
            pltpu.VMEM((rows, width), jnp.bfloat16),
            pltpu.SemaphoreType.DMA((2,)),
        ],
        compiler_params=params,
    )(mixed, blocks))


def solution(mesh):
    placed = (
        P(None, "tp", None),
        P(None, "tp", "kvp", None),
        P(None, "tp", "kvp", None),
        P(),
        P("tp", "kvp"),
        P(None, "kvp"),
        P("kvp"),
        P("kvp", "tp"),
        P("kvp", "tp"),
    )
    return jax.shard_map(
        local,
        mesh=mesh,
        in_specs=placed,
        out_specs=(P(None, "kvp"), P(None, "tp")),
        check_vma=False,
    )
```
